32 devices in a mesh: row: 4 (over y, x), rhs: 8 (over z, core).
Axes of the slice: x: 2, y: 2, z: 4, core: 2. Of those that a mesh axis runs over, the one named last changes fastest.
Arguments:
- right_side: float32 [8, 4, 256, 8192], P(None, 'row', None, 'rhs'), may hold values from -6 to 6
- factor: float32 [8, 4, 256, 1024], P(None, 'row', None, 'rhs'), may hold values from -0.09375 to 0.09375
- inverses: float32 [4, 256, 256], replicated, may hold values from -1 to 2, as said below
- far_operator: float32 [512, 8, 4, 256], P(None, None, 'row'), may hold values from -0.09375 to 0.09375
Outputs:
- solved_rhs: float32 [8, 4, 256, 8192], P(None, 'row', None, 'rhs')
- far_field: float32 [512, 8192], P('row', 'rhs')
The draws below stay inside these ranges and needn't reach their ends.
Inputs may be any that keep to these rules, and one draw needn't show every extreme that they name: inverses of well-conditioned diagonal blocks.
All inputs are finite; a program needn't handle non-finite values.
Results may differ from the reference program's by a relative error of at most 0.0001.
Values sent between devices are 32-bit elements; how exact they have to be, the bound alone decides.
A program may use at most 128 MiB of HBM per device.

```python
import math
import jax
import jax.numpy as jnp
from jax import lax

BLOCK = 256
PANELS = 4
ANGLES = 512
BLK_DEV = 8
BLOCKS = 32
ROWS = 8192
COLS = 8192
N_ROW = 4


def draw_inverses(key, part):
    base = jnp.eye(BLOCK, dtype=jnp.float32)[None]
    noise = jnp.clip(jax.random.normal(key, (PANELS, BLOCK, BLOCK), jnp.float32), -4.0, 4.0) * (0.6 / math.sqrt(BLOCK))
    return base + noise


def with_spikes(entries, rng, source, target, parts, factor):
    owner, partner = [(jnp.arange(entries.shape[position]) // (entries.shape[position] // parts)).reshape([-1 if axis == position else 1 for axis in range(entries.ndim)]) for position in (source, target)]
    chosen = jax.random.permutation(rng, parts)[partner]
    strong = (owner == chosen) | (owner == (partner + parts // 2) % parts)
    return jnp.where(strong, factor * entries, entries)


def level_of(rng, dims, pieces, smallest, largest):
    loudness, own = 1.0, jax.random.fold_in(rng, 6)
    for axis_at, shards_of in pieces:
        heights = jnp.exp(jax.random.uniform(jax.random.fold_in(own, axis_at), (shards_of,), jnp.float32, smallest / len(pieces), largest / len(pieces)))
        loudness = loudness * jnp.repeat(heights, dims[axis_at] // shards_of).reshape([-1 if axis == axis_at else 1 for axis in range(len(dims))])
    return loudness


def centred(own_key, extent, width, limit, shards=(), held_as=jnp.bfloat16):
    entries = jax.random.normal(own_key, extent, jnp.float32) * width
    if len(shards) > 0:
        entries = level_of(own_key, extent, shards, -0.22, 0.18) * entries
    return jnp.clip(entries, min=-limit, max=limit).astype(held_as)


def noise_with(rng, dims, deviation, bound, split, heavy, held_as=jnp.bfloat16):
    entries = deviation * jax.random.normal(rng, dims, jnp.float32)
    if split:
        entries = entries * level_of(rng, dims, split, -0.22, 0.18)
    return jnp.clip(with_spikes(entries, jax.random.fold_in(rng, 3), *heavy), -bound, bound).astype(held_as)


def setup_inputs(seed: int = 0) -> dict:
    key_list = jax.random.split(jax.random.key(seed), 5)
    return {
        "right_side": centred(key_list[0], (BLK_DEV, N_ROW, BLOCK, COLS), 1.0, 6.0, ((1, 4), (3, 8)), jnp.float32),
        "factor": centred(key_list[1], (BLK_DEV, N_ROW, BLOCK, PANELS * BLOCK), (4 * PANELS * BLOCK) ** -0.5, 0.09375, ((1, 4), (3, 8)), jnp.float32),
        "inverses": draw_inverses(jax.random.fold_in(key_list[4], 71), 0),
        "far_operator": noise_with(key_list[3], (ANGLES, BLK_DEV, N_ROW, BLOCK), ROWS ** -0.5, 0.09375, ((2, 4),), (2, 0, 4, 2.0), jnp.float32),
    }


def product(left_side, right_side):
    return jnp.dot(left_side, right_side, precision=lax.Precision.HIGHEST, preferred_element_type=jnp.float32)


def reference(right_side, factor, inverses, far_operator):
    block_width = BLOCK
    blocks_all = right_side.reshape(BLOCKS, BLOCK, COLS)
    rows_all = factor.reshape(BLOCKS, BLOCK, PANELS * BLOCK)
    solved = []
    for panel_index in range(PANELS):
        current = blocks_all[panel_index]
        for earlier in range(panel_index):
            current = current - product(rows_all[panel_index][:, earlier * block_width:(earlier + 1) * block_width], solved[earlier])
        solved.append(product(inverses[panel_index], current))
    stacked = jnp.concatenate(solved, 0)
    remaining = blocks_all[PANELS:].reshape(-1, COLS) - product(rows_all[PANELS:].reshape(-1, PANELS * BLOCK), stacked)
    flat_rhs = jnp.concatenate([stacked, remaining], 0)
    solved_rhs = flat_rhs.reshape(right_side.shape)
    far_field = product(far_operator.reshape(ANGLES, ROWS), flat_rhs)
    return solved_rhs, far_field
```

```python
import functools

import jax
import jax.numpy as jnp
from jax import lax
from jax.experimental import pallas as pl
from jax.experimental.pallas import tpu as pltpu
from jax.sharding import PartitionSpec as P

F32, BF16 = jnp.float32, jnp.bfloat16
UP, DOWN, PAIR = 0, 1, 2


def split(values):
    high = values.astype(BF16)
    return high, (values - high.astype(F32)).astype(BF16)


def dot3(left, right):
    dot = functools.partial(jnp.dot, preferred_element_type=F32)
    return dot(left[0], right[0]) + (dot(left[0], right[1]) + dot(left[1], right[0]))


def kernel(
    rows, rhs, rhs_hbm, fac_hbm, inv_hbm, far_hbm, out_hbm, far_out,
    total, panel, far, lead, lead_fac, inv, x_hi, x_lo, part, part_in, mix, mix_in, mixed,
    load_sem, far_sem, out_sem, send_sem, recv_sem, lead_send, lead_recv, lf_send, lf_recv,
    part_send, part_recv, mix_send, mix_recv,
):
    panels, width = inv.shape[:2]
    blocks, _, columns = total.shape
    share = fac_hbm.shape[3]
    angles = far.shape[1]
    mine = angles // rows
    chain = rhs // 2
    per_panel = width // share
    row, col = lax.axis_index("row"), lax.axis_index("rhs")
    pos, core = col // 2, col % 2
    pair = 2 * pos + 1 - core
    is_lead = row < panels
    half = columns // 2
    G = blocks

    def peer(step):
        out, bit = 0, 1
        while bit < rows:
            out = out + ((row // bit + (step // bit) % 2) % 2) * bit
            bit *= 2
        return out

    def remote(src, dst, send, recv, device):
        return pltpu.make_async_remote_copy(
            src_ref=src, dst_ref=dst, send_sem=send, recv_sem=recv,
            device_id=device, device_id_type=pl.DeviceIdType.MESH,
        )

    barrier = pltpu.get_barrier_semaphore()

    def greet(device):
        pl.semaphore_signal(barrier, inc=1, device_id=device, device_id_type=pl.DeviceIdType.MESH)

    loads = [
        pltpu.make_async_copy(fac_hbm.at[:, 0], panel.at[col], load_sem.at[0]),
        pltpu.make_async_copy(rhs_hbm.at[:, 0], total, load_sem.at[1]),
        pltpu.make_async_copy(inv_hbm, inv, load_sem.at[2]),
    ]
    far_loads = [
        pltpu.make_async_copy(far_hbm.at[:, i, 0], far.at[i], far_sem.at[i]) for i in range(blocks)
    ]
    loads[0].start()
    for load in far_loads:
        load.start()
    loads[1].start()
    loads[2].start()

    for step in range(1, rows):
        greet((peer(step), col))
    greet((row, pair))
    has_up, has_down = pos < chain - 1, pos > 0

    @pl.when(has_up)
    def _():
        greet((row, col + 2))

    @pl.when(has_down)
    def _():
        greet((row, col - 2))

    pl.semaphore_wait(
        barrier, rows + jnp.where(has_up, 1, 0) + jnp.where(has_down, 1, 0)
    )

    def slot(src, b, is_mix):
        return mixed.at[src] if is_mix else panel.at[src, b]

    def chain_copy(kind, src, b, is_mix, from_ref=None):
        here = slot(src, b, is_mix)
        device = (row, {UP: col + 2, DOWN: col - 2, PAIR: pair}[kind])
        return remote(
            here if from_ref is None else from_ref, here,
            send_sem.at[kind, src, b], recv_sem.at[src, b], device,
        )

    def needed(src, b, is_mix):
        if is_mix or (isinstance(b, int) and b > 0):
            return True
        used = ((src * share) // width < row) | jnp.logical_not(is_lead)
        if isinstance(b, int):
            return used
        return used | (b > 0)

    def own_send(b, is_mix=False, from_ref=None):
        ok = needed(col, b, is_mix)

        @pl.when(has_up & ok)
        def _():
            chain_copy(UP, col, b, is_mix, from_ref).start()

        @pl.when(has_down & ok)
        def _():
            chain_copy(DOWN, col, b, is_mix, from_ref).start()

        @pl.when(ok)
        def _():
            chain_copy(PAIR, col, b, is_mix, from_ref).start()

    def arrive(src, b, is_mix):
        chain_copy(PAIR, src, b, is_mix).wait_recv()

    def relay(distance, b, is_mix=False, lead_block=False):
        for sign, kind, more in ((-1, UP, has_up), (1, DOWN, has_down)):
            at = pos + sign * distance
            src = 2 * at + core

            @pl.when((at >= 0) & (at < chain) & needed(src, 0 if lead_block else 1, is_mix))
            def _():
                arrive(src, b, is_mix)

                @pl.when(more)
                def _():
                    chain_copy(kind, src, b, is_mix).start()

                chain_copy(PAIR, src, b, is_mix).start()

    def send_lead_fac(src):
        @pl.when(is_lead & ((src * share) // width < row))
        def _():
            for step in range(1, rows):
                remote(
                    panel.at[src, 0], lead_fac.at[row, src], lf_send.at[step, src],
                    lf_recv.at[row, src], (peer(step), col),
                ).start()

    def rhs_part(q):
        return rhs_hbm.at[0, 0, :, pl.ds(q * half, half)]

    def lead_part(k, q):
        return lead.at[k, :, pl.ds(q * half, half)]

    hops = (1, 2) if rows == 4 else tuple(range(1, rows))

    def lead_copy(step, q):
        return remote(
            rhs_part(q), lead_part(row, q), lead_send.at[step, q], lead_recv.at[row, q],
            (peer(step), col),
        )

    def pass_on(q):
        source, to = (peer(1), 2) if q == 0 else (peer(2), 1)
        return remote(
            lead_part(source, q), lead_part(source, q), lead_send.at[3, q],
            lead_recv.at[source, q], (peer(to), col),
        )

    own_send(0, from_ref=fac_hbm.at[0, 0])

    @pl.when(is_lead)
    def _():
        for order in range(2):
            for n, step in enumerate(hops):
                lead_copy(step, (order + n) % 2).start()
        for q in range(2):
            pltpu.make_async_copy(rhs_part(q), lead_part(row, q), lead_recv.at[row, q]).start()

    for b in range(1, blocks):
        own_send(b, from_ref=fac_hbm.at[b, 0])

    loads[0].wait()
    for load in far_loads:
        load.wait()
    send_lead_fac(col)
    start = col * share
    for t in range(per_panel):
        @pl.when(is_lead & (start // width == row) & ((start % width) // share == t))
        def _():
            mix[...] = far[0, :, t * share : (t + 1) * share]

    @pl.when(jnp.logical_not(is_lead & (start // width == row)))
    def _():
        mix[...] = jnp.zeros_like(mix)

    def mix_block(b):
        mix[...] -= dot3(split(far[b]), split(panel[col, b]))

    @pl.when(jnp.logical_not(is_lead))
    def _():
        mix_block(0)

    @pl.loop(1, blocks)
    def _(b):
        mix_block(b)

    def strip(ref, index):
        return ref.at[pl.ds(pl.multiple_of(index * mine, mine), mine)]

    def mix_copy(step):
        return remote(
            strip(mix, peer(step)), mix_in.at[row], mix_send.at[step], mix_recv.at[row],
            (peer(step), col),
        )

    for step in range(1, rows):
        mix_copy(step).start()

    loads[1].wait()
    part[...] = jnp.zeros_like(part)

    def part_block(b):
        left = split(far[b])

        @pl.loop(0, columns // width)
        def _(n):
            at = pl.ds(pl.multiple_of(n * width, width), width)
            part[:, at] += dot3(left, split(total[b, :, at]))

    @pl.when(jnp.logical_not(is_lead))
    def _():
        part_block(0)

    def lead_step(distance):
        relay(distance, 0, lead_block=True)
        for sign in (-1, 1):
            at = pos + sign * distance
            src = 2 * at + core

            @pl.when((at >= 0) & (at < chain))
            def _():
                send_lead_fac(src)

    cuts = [1 + ((blocks - 1) * n) // (chain - 1) for n in range(chain)]
    for n in range(chain - 1):
        @pl.loop(cuts[n], cuts[n + 1])
        def _(b):
            part_block(b)

        lead_step(n + 1)

    for step in range(1, rows):
        source = peer(step)
        remote(
            mix_in.at[source], mix_in.at[source], mix_send.at[step], mix_recv.at[source], (row, pair)
        ).wait_recv()
    value = mix[pl.ds(pl.multiple_of(row * mine, mine), mine), :]
    for step in range(1, rows):
        value = value + mix_in[peer(step)]
    mixed[col] = value
    own_send(G, True)

    def wait_lead(k, q):
        remote(
            lead_part(k, q), lead_part(k, q), lead_send.at[0, q], lead_recv.at[k, q], (row, pair)
        ).wait_recv()

    if rows == 4:
        for q in range(2):
            wait_lead(peer(1) if q == 0 else peer(2), q)
            pass_on(q).start()

    @pl.loop(1, blocks)
    def _(b):
        relay(1, b)

    relay(1, G, True)

    def lf_wait(k, src):
        remote(
            lead_fac.at[k, src], lead_fac.at[k, src], lf_send.at[0, src], lf_recv.at[k, src], (row, pair)
        ).wait_recv()

    def lf_pair(k, src):
        return remote(
            lead_fac.at[k, src], lead_fac.at[k, src], lf_send.at[rows + k, src], lf_recv.at[k, src],
            (row, pair),
        )

    for k in range(1, panels):
        for at in range(k * per_panel // 2):
            src = 2 * at + core

            @pl.when(row != k)
            def _():
                lf_wait(k, src)
                lf_pair(k, src).start()

    early = 1 + (blocks - 1) // 2
    if chain > 2:
        @pl.loop(1, early)
        def _(b):
            relay(2, b)

    for k in range(1, panels):
        for at in range(k * per_panel // 2):
            src = 2 * at + 1 - core

            @pl.when(row != k)
            def _():
                lf_wait(k, src)

            @pl.when(row == k)
            def _():
                arrive(src, 0, False)
                for each in (src, 2 * at + core):
                    lead_fac[k, each] = panel[each, 0]

    loads[2].wait()
    for q in range(2):
        for k in range(panels):
            if rows == 4:
                @pl.when(k != (peer(1) if q == 0 else peer(2)))
                def _():
                    @pl.when(k != row)
                    def _():
                        wait_lead(k, q)
            else:
                @pl.when(k != row)
                def _():
                    wait_lead(k, q)

            @pl.when(k == row)
            def _():
                pltpu.make_async_copy(rhs_part(q), lead_part(k, q), lead_recv.at[k, q]).wait()

    def solve(n):
        at = pl.ds(pl.multiple_of(n * width, width), width)
        for k in range(panels):
            pending = lead[k, :, at]
            for j in range(k):
                left = jnp.concatenate(
                    [lead_fac[k, j * per_panel + t] for t in range(per_panel)], 1
                )
                above = pl.ds(j * width, width)
                pending = pending - dot3(split(left), (x_hi[above, at], x_lo[above, at]))
            value = dot3(split(inv[k]), split(pending))
            high, low = split(value)
            x_hi[pl.ds(k * width, width), at] = high
            x_lo[pl.ds(k * width, width), at] = low

            @pl.when(row == k)
            def _():
                total[0, :, at] = value

    @pl.loop(0, columns // width)
    def _(n):
        solve(n)

    def part_copy(step):
        return remote(
            strip(part, peer(step)), part_in.at[row], part_send.at[step], part_recv.at[row],
            (peer(step), col),
        )

    for step in range(1, rows):
        part_copy(step).start()

    span = 2 * share

    def apply(at, b):
        left = split(jnp.concatenate([panel[2 * at, b], panel[2 * at + 1, b]], 1))
        rows_at = pl.ds(pl.multiple_of(at * span, span), span)

        @pl.loop(0, 2)
        def _(n):
            here = pl.ds(pl.multiple_of(n * half, half), half)
            total[b, :, here] -= dot3(left, (x_hi[rows_at, here], x_lo[rows_at, here]))

    def update(distance, b):
        for sign in (-1, 1) if distance else (1,):
            at = pos + sign * distance

            @pl.when((at >= 0) & (at < chain))
            def _():
                arrive(2 * at + 1 - core, b, False)
                apply(at, b)

    def out_copy(b):
        return pltpu.make_async_copy(total.at[b], out_hbm.at[b, 0], out_sem.at[b])

    @pl.loop(1, blocks)
    def _(b):
        update(0, b)
        update(1, b)
        if chain > 2:
            @pl.when(b >= early)
            def _():
                relay(2, b)

    relay(2, G, True)
    for distance in range(3, chain - 1):
        @pl.loop(1, blocks)
        def _(b):
            update(distance - 1, b)
            relay(distance, b)

        relay(distance, G, True)

    @pl.when(jnp.logical_not(is_lead))
    def _():
        for at in range(chain):
            arrive(2 * at + 1 - core, 0, False)
            apply(at, 0)

    out_copy(0).start()
    last = chain - 1
    relay(last, G, True)

    for at in range(chain):
        arrive(2 * at + 1 - core, G, True)
    for step in range(1, rows):
        source = peer(step)
        remote(
            part_in.at[source], part_in.at[source], part_send.at[step], part_recv.at[source], (row, pair)
        ).wait_recv()

    @pl.loop(0, columns // width)
    def _(n):
        here = pl.ds(pl.multiple_of(n * width, width), width)
        value = part[pl.ds(pl.multiple_of(row * mine, mine), mine), here]
        for step in range(1, rows):
            value = value + part_in[peer(step), :, here]
        for at in range(chain):
            left = split(jnp.concatenate([mixed[2 * at], mixed[2 * at + 1]], 1))
            rows_at = pl.ds(at * span, span)
            value = value + dot3(left, (x_hi[rows_at, here], x_lo[rows_at, here]))
        far_out[:, here] = value

    @pl.loop(1, blocks + 1)
    def _(b):
        @pl.when(b < blocks)
        def _():
            update(last - 1, b)
            relay(last, b)

        @pl.when(b > 1)
        def _():
            update(last, b - 1)
            out_copy(b - 1).start()

    for src_at in range(chain):
        @pl.loop(0, blocks)
        def _(b):
            drain(chain_copy, needed, 2 * src_at + core, b, False, pos, src_at, has_up, has_down)

        drain(chain_copy, needed, 2 * src_at + core, G, True, pos, src_at, has_up, has_down)

        other = 2 * src_at + 1 - core
        waited = src_at < panels * per_panel // 2

        @pl.when(is_lead & ((other * share) // width < row))
        def _():
            if not waited:
                arrive(other, 0, False)

        @pl.when(is_lead & (((2 * src_at + core) * share) // width < row))
        def _():
            for step in range(1, rows):
                remote(
                    panel.at[2 * src_at + core, 0], panel.at[2 * src_at + core, 0],
                    lf_send.at[step, 2 * src_at + core], lf_recv.at[0, 0], (row, pair),
                ).wait_send()

    for k in range(1, panels):
        for at in range(k * per_panel // 2):
            @pl.when(row != k)
            def _():
                lf_pair(k, 2 * at + core).wait_send()

    @pl.when(is_lead)
    def _():
        for q in range(2):
            for step in hops:
                lead_copy(step, q).wait_send()
    if rows == 4:
        for q in range(2):
            pass_on(q).wait_send()
    for step in range(1, rows):
        mix_copy(step).wait_send()
        part_copy(step).wait_send()

    @pl.loop(0, blocks)
    def _(b):
        out_copy(b).wait()


def drain(chain_copy, needed, src, b, is_mix, pos, src_at, has_up, has_down):
    ok = needed(src, b, is_mix)

    @pl.when(has_up & (src_at <= pos) & ok)
    def _():
        chain_copy(UP, src, b, is_mix).wait_send()

    @pl.when(has_down & (src_at >= pos) & ok)
    def _():
        chain_copy(DOWN, src, b, is_mix).wait_send()

    @pl.when(ok)
    def _():
        chain_copy(PAIR, src, b, is_mix).wait_send()


def shards(rows, rhs, right_side, factor, inverses, far_operator):
    panels, width = inverses.shape[:2]
    blocks, columns = right_side.shape[0], right_side.shape[3]
    angles, share = far_operator.shape[0], factor.shape[3]
    mine = angles // rows
    vmem, dma = pltpu.VMEM, pltpu.SemaphoreType.DMA
    return pl.pallas_call(
        functools.partial(kernel, rows, rhs),
        out_shape=(
            jax.ShapeDtypeStruct(right_side.shape, F32),
            jax.ShapeDtypeStruct((mine, columns), F32),
        ),
        in_specs=[pl.BlockSpec(memory_space=pl.ANY)] * 4,
        out_specs=(
            pl.BlockSpec(memory_space=pl.ANY),
            pl.BlockSpec(memory_space=pltpu.VMEM),
        ),
        scratch_shapes=[
            vmem((blocks, width, columns), F32),
            vmem((rhs, blocks, width, share), F32),
            vmem((blocks, angles, width), F32),
            vmem((panels, width, columns), F32),
            vmem((panels, rhs, width, share), F32),
            vmem((panels, width, width), F32),
            vmem((panels * width, columns), BF16),
            vmem((panels * width, columns), BF16),
            vmem((angles, columns), F32),
            vmem((rows, mine, columns), F32),
            vmem((angles, share), F32),
            vmem((rows, mine, share), F32),
            vmem((rhs, mine, share), F32),
            dma((3,)),
            dma((blocks,)),
            dma((blocks,)),
            dma((3, rhs, blocks + 1)),
            dma((rhs, blocks + 1)),
            dma((max(rows, 4), 2)),
            dma((rows, 2)),
            dma((rows + panels, rhs)),
            dma((panels, rhs)),
            dma((rows,)),
            dma((rows,)),
            dma((rows,)),
            dma((rows,)),
        ],
        compiler_params=pltpu.CompilerParams(
            collective_id=0, has_side_effects=True, vmem_limit_bytes=60 * 2**20
        ),
    )(right_side, factor, inverses, far_operator)


def solution(mesh):
    return jax.shard_map(
        functools.partial(shards, mesh.shape["row"], mesh.shape["rhs"]),
        mesh=mesh,
        in_specs=(
            P(None, "row", None, "rhs"),
            P(None, "row", None, "rhs"),
            P(),
            P(None, None, "row", None),
        ),
        out_specs=(P(None, "row", None, "rhs"), P("row", "rhs")),
        check_vma=False,
    )
```
